32 devices in a mesh: groups: 2 (over y), blk: 4 (over z), term: 2 (over x), rep: 2 (over core).
Axes of the slice: x: 2, y: 2, z: 4, core: 2. Of those that a mesh axis runs over, the one named last changes fastest.
Arguments:
- wavefunction: bfloat16 [2048, 512], P(('groups', 'blk'), 'rep'), parts along dimension 0, may hold values from -6 to 6
- left_env: bfloat16 [2048, 16, 512], P(('groups', 'blk'), 'term'), parts along dimension 0, may hold values from -0.0625 to 0.0625
- right_env: bfloat16 [2048, 16, 512], P(('groups', 'blk'), 'term', 'rep'), parts along dimension 0, may hold values from -0.25 to 0.25
- sources: int32 [32, 2], P('groups'), parts along dimension 0, may hold values from 0 to 1
- live_dims: int32 [4, 2], P('groups'), parts along dimension 0, may hold values from 64 to 512, as said below
Outputs:
- next_basis: bfloat16 [2048, 512], P(('groups', 'blk', 'term', 'rep')), parts along dimension 0
- second_image: bfloat16 [2048, 512], P(('groups', 'blk', 'term', 'rep')), parts along dimension 0
- projection: float32 [4], P('groups'), parts along dimension 0
The draws below stay inside these ranges and needn't reach their ends.
There are 2 independent parts, one for each index of `groups`. The reference program is written for one: setup_inputs(seed, part) draws one part's arguments, and reference() takes and returns one part's arrays. A program takes and returns all parts, laid end to end along the dimension named above; each array names one. Nothing has to cross between parts.
Inputs may be any that keep to these rules, and one draw needn't show every extreme that they name: `live_dims`: live rows and columns of each sector block; in some block both equal 512.
All inputs are finite; a program needn't handle non-finite values.
Results may differ from the reference program's by a relative error of at most 0.009.
Values may be sent and summed in bfloat16 or wider, within the bound.
A program may use at most 64 MiB of HBM per device.

```python
import jax
import jax.numpy as jnp
from jax import lax

M = 512
BLOCKS = 2
TERMS = 16


def draw_live_dims(key, part):
    key = jax.random.fold_in(key, 17)
    first_key, second_key = jax.random.split(key)
    drawn = jax.random.randint(first_key, (BLOCKS, 2), M // 8, M + 1)
    widest = jax.random.randint(second_key, (), 0, BLOCKS)
    positions = jnp.arange(BLOCKS)[:, None]
    return jnp.where(positions == widest, M, drawn).astype(jnp.int32)


def touch_ends(result, own_key, low, largest):
    dims = result.shape
    spot = [jax.random.randint(jax.random.fold_in(own_key, axis), (), 0, dims[axis]) for axis in range(len(dims))]
    result = result.at[tuple(spot)].set(low)
    longest = dims.index(max(dims))
    spot[longest] = (spot[longest] + 1) % dims[longest]
    return result.at[tuple(spot)].set(largest)


def shard_levels(stream_key, extent, shards, smallest, largest):
    def one(position, shards_of):
        steps = jax.random.uniform(jax.random.fold_in(jax.random.fold_in(stream_key, 6), position), (shards_of,), jnp.float32, smallest / len(shards), largest / len(shards))
        return jnp.repeat(jnp.exp(steps), extent[position] // shards_of).reshape((-1,) + (1,) * (len(extent) - position - 1))

    factor_of = one(*shards[0])
    for cut in shards[1:]:
        factor_of = factor_of * one(*cut)
    return factor_of


def noise(key, extent, deviation, most, pieces=(), kind=jnp.bfloat16):
    gain = shard_levels(key, extent, pieces, -0.22, 0.18) if pieces else 1.0
    values = jax.random.normal(key, extent, jnp.float32) * deviation * gain
    return jnp.minimum(jnp.maximum(values, -most), most).astype(kind)


def setup_inputs(seed: int = 0, part: int = 0) -> dict:
    streams_of = jax.random.split(jax.random.key(seed), 6)
    own_keys = jax.random.split(jax.random.fold_in(streams_of[5], part), 6)
    return {
        "wavefunction": noise(own_keys[0], (BLOCKS * M, M), 1.0, 6.0, ((0, 4), (1, 2))),
        "left_env": noise(own_keys[1], (BLOCKS * M, TERMS, M), (M * TERMS) ** -0.5, 0.0625, ((0, 4), (1, 2))),
        "right_env": noise(own_keys[2], (BLOCKS * M, TERMS, M), M ** -0.5, 0.25, ((0, 4), (1, 2), (2, 2))),
        "sources": touch_ends(jax.random.randint(own_keys[3], (TERMS, BLOCKS), 0, BLOCKS), jax.random.fold_in(own_keys[3], 1), 0, BLOCKS - 1).astype(jnp.int32),
        "live_dims": draw_live_dims(jax.random.fold_in(jax.random.fold_in(streams_of[5], part), 71), part),
    }


EPSILON = 1e-06

def sector_live_mask(live_dims):
    positions = jnp.arange(M, dtype=jnp.int32)
    row_live = positions[None, :] < live_dims[:, 0:1]
    col_live = positions[None, :] < live_dims[:, 1:2]
    return row_live[:, :, None] & col_live[:, None, :]

def apply_hamiltonian(vector, left_env, right_env, sources, sector_live):
    masked = jnp.where(sector_live, vector.reshape(BLOCKS, M, M), jnp.zeros((), jnp.bfloat16))
    left_blocks = left_env.reshape(BLOCKS, M, TERMS, M)
    right_blocks = right_env.reshape(BLOCKS, M, TERMS, M)

    def one_block(block_index):
        sources_now = masked[sources[:, block_index]]
        halfway = jnp.einsum('awc,wcb->wab', left_blocks[block_index].astype(jnp.float32), sources_now.astype(jnp.float32)).astype(jnp.bfloat16)
        return jnp.einsum('wab,dwb->ad', halfway.astype(jnp.float32), right_blocks[block_index].astype(jnp.float32))
    products = lax.map(one_block, jnp.arange(BLOCKS, dtype=jnp.int32))
    products = jnp.where(sector_live, products, jnp.zeros((), jnp.float32))
    return products.reshape(BLOCKS * M, M)

def reference(wavefunction, left_env, right_env, sources, live_dims):
    sector_live = sector_live_mask(live_dims)
    start_vector = jnp.where(sector_live, wavefunction.reshape(BLOCKS, M, M), jnp.zeros((), jnp.bfloat16)).reshape(BLOCKS * M, M)
    start_float = start_vector.astype(jnp.float32)
    first_image = apply_hamiltonian(start_vector, left_env, right_env, sources, sector_live)
    self_product = jnp.sum(start_float * start_float)
    cross_product = jnp.sum(start_float * first_image)
    rayleigh = cross_product / (self_product + EPSILON)
    residual = first_image - rayleigh * start_float
    residual_square = jnp.sum(residual * residual)
    entry_count = jnp.float32(BLOCKS * M * M)
    norm_scale = lax.rsqrt(residual_square / entry_count + EPSILON)
    next_basis = (residual * norm_scale).astype(jnp.bfloat16)
    image_float = apply_hamiltonian(next_basis, left_env, right_env, sources, sector_live)
    image_correlation = jnp.sum(next_basis.astype(jnp.float32) * image_float)
    projection = jnp.stack([rayleigh, image_correlation / entry_count])
    return (next_basis, image_float.astype(jnp.bfloat16), projection)
```

```python
import functools

import jax
import jax.numpy as jnp
from jax import lax
from jax.experimental import pallas as pl
from jax.experimental.pallas import tpu as pltpu
from jax.sharding import PartitionSpec as P

EPSILON = 1e-06
MESH = pl.DeviceIdType.MESH
F32 = jnp.float32
BF16 = jnp.bfloat16


def kernel(
    B, T, R, blocks,
    wf, left, right, sources, live,
    nb_out, img_out, proj_out,
    left_raw, left_f, left_w, right_raw, right_got, right_f, right_w,
    v1, vm, v2, sbuf, half, part1, part2, red1, red2, f_ref, fb, sc_a, sc_b, sc_c, sc_d,
    loc_sem, rsend, rrecv, v_send, v_recv, vx_send, vx_recv, s_sem,
    p1_send, p1_recv, p2_send, p2_recv, g_send, g_recv, gx_send, gx_recv,
    sc_send, sc_recv,
):
    TR = T * R
    b, t, r = lax.axis_index("blk"), lax.axis_index("term"), lax.axis_index("rep")
    slot = t * R + r
    rows, W, M = left.shape
    ro = rows // TR
    hc = M // R
    qc = M // 4
    own, u = b // 2, b % 2

    def copy(src, dst, ss, rs, bb, tt, rr):
        return pltpu.make_async_remote_copy(
            src_ref=src, dst_ref=dst, send_sem=ss, recv_sem=rs,
            device_id={"blk": bb, "term": tt, "rep": rr}, device_id_type=MESH)

    def zpeer(k):
        return lax.rem(b + k, B)

    def zfrom(k):
        return lax.rem(b - k + B, B)

    def speer(k):
        p = lax.rem(slot + k, TR)
        return p // R, lax.rem(p, R)

    barrier = pltpu.get_barrier_semaphore()
    for k in range(B):
        for j in range(R):
            if k or j:
                pl.semaphore_signal(barrier, inc=1, device_id={"blk": zpeer(k), "term": t, "rep": lax.rem(r + j, R)}, device_id_type=MESH)
    for k in range(1, TR):
        tt, rr = speer(k)
        pl.semaphore_signal(barrier, inc=1, device_id={"blk": b, "term": tt, "rep": rr}, device_id_type=MESH)

    lcopy = pltpu.make_async_copy(left, left_raw, loc_sem.at[0])
    lcopy.start()
    rcopy = pltpu.make_async_copy(right, right_raw, loc_sem.at[1])
    rcopy.start()
    pl.semaphore_wait(barrier, B * R - 1 + TR - 1)

    def piece(buf, bb, start, n):
        return buf.at[bb // 2, pl.ds((bb % 2) * TR + start, n)]

    vz = []
    for k in range(1, B):
        c = copy(wf.at[pl.ds(t * R, R)], piece(v1, b, t * R, R), v_send.at[k - 1], v_recv.at[k - 1], zpeer(k), t, r)
        c.start()
        vz.append(c)
    mine = [copy(wf.at[t * R + lax.rem(r + 1, R)], sbuf, s_sem.at[0], s_sem.at[1], b, t, lax.rem(r + 1, R))]
    mine[0].start()
    other = b + 1 - 2 * u
    chunk = rows // 2
    rz = []
    for c in range(2):
        d = pl.ds(c * chunk, chunk)
        cp = copy(right.at[d], right_got.at[d], rsend.at[c], rrecv.at[c], other, t, r)
        cp.start()
        rz.append(cp)

    v1[own, pl.ds(u * TR, TR)] = wf[...]

    lcopy.wait()
    left_f[...] = left_raw[...].astype(F32)
    for w in range(W):
        left_w[w] = left_f[:, w, :].astype(BF16)
    rcopy.wait()
    right_f[...] = right_raw[...].astype(F32)
    for w in range(W):
        right_w[u, :, w * hc:(w + 1) * hc] = right_f[:, w, :].astype(BF16)

    vx = []
    for k in range(1, B):
        src = zfrom(k)
        here = piece(v1, src, t * R, R)
        copy(here, here, v_send.at[k - 1], v_recv.at[k - 1], src, t, r).wait_recv()
        for j in range(1, T):
            c = copy(here, here, vx_send.at[k - 1, j - 1], vx_recv.at[k - 1, j - 1], b, lax.rem(t + j, T), r)
            c.start()
            vx.append(c)
    for k in range(1, B):
        src = zfrom(k)
        for j in range(1, T):
            tt = lax.rem(t - j + T, T)
            there = piece(v1, src, tt * R, R)
            copy(there, there, vx_send.at[k - 1, j - 1], vx_recv.at[k - 1, j - 1], b, tt, r).wait_recv()
    row_of = lax.broadcasted_iota(jnp.int32, (2 * TR, ro, hc), 0) * ro + lax.broadcasted_iota(jnp.int32, (2 * TR, ro, hc), 1)
    col_of = lax.broadcasted_iota(jnp.int32, (2 * TR, ro, hc), 2) + r * hc

    @pl.loop(0, blocks)
    def _(k):
        ok = (row_of < live[k, 0]) & (col_of < live[k, 1])
        vm[k] = jnp.where(ok, v1[k].astype(F32), 0.0).astype(BF16)

    def halfway(v):
        for w in range(W):
            src = sources[t * W + w, own]
            x = v[src].reshape(M, hc)
            half[:, w * hc:(w + 1) * hc] = jnp.dot(left_w[w], x, preferred_element_type=F32).astype(BF16)

    def product(h, lo, n):
        return lax.dot_general(half[...], right_w[h, lo:lo + n, :], (((1,), (1,)), ((), ())), preferred_element_type=F32)

    def scatter(part, red, sends, recvs, q, p):
        out = []
        for k in range(1, TR):
            tt, rr = speer(k)
            c = copy(part.at[q, pl.ds(lax.rem(slot + k, TR) * ro, ro)], red.at[q, k - 1],
                     sends.at[p, k - 1], recvs.at[p, k - 1], b, tt, rr)
            c.start()
            out.append(c)
        return out

    out_row = lax.broadcasted_iota(jnp.int32, (ro, M), 0) + u * rows + slot * ro
    out_col = lax.broadcasted_iota(jnp.int32, (ro, M), 1)
    out_live = (out_row < live[own, 0]) & (out_col < live[own, 1])

    def gathered(part, red):
        got = []
        for q in range(4):
            x = part[q, pl.ds(slot * ro, ro), :]
            for k in range(1, TR):
                x = x + red[q, k - 1]
            got.append(x)
        return jnp.where(out_live, jnp.concatenate(got, axis=1), 0.0)

    def await_all(copies):
        for c in copies:
            c.wait()

    halfway(vm)
    x = product(u, 0, 2 * qc)
    part1[2 * u] = x[:, :qc]
    part1[2 * u + 1] = x[:, qc:]
    p1 = scatter(part1, red1, p1_send, p1_recv, 2 * u, 0)
    p1 += scatter(part1, red1, p1_send, p1_recv, 2 * u + 1, 1)
    for c in range(2):
        rz[c].wait()
        lo = c * chunk
        right_f[lo:lo + chunk] = right_got[lo:lo + chunk].astype(F32)
        for w in range(W):
            right_w[1 - u, lo:lo + chunk, w * hc:(w + 1) * hc] = right_f[lo:lo + chunk, w, :].astype(BF16)
        part1[2 * (1 - u) + c] = product(1 - u, lo, chunk)
        p1 += scatter(part1, red1, p1_send, p1_recv, 2 * (1 - u) + c, 2 + c)

    mine[0].wait()
    kept = wf[slot]
    for_r0 = jnp.concatenate([kept, sbuf[...]], axis=1).astype(F32)
    for_r1 = jnp.concatenate([sbuf[...], kept], axis=1).astype(F32)
    start = jnp.where(out_live, jnp.where(r == 0, for_r0, for_r1), 0.0)
    await_all(p1)
    first = gathered(part1, red1)
    f_ref[...] = first

    for j in range(R):
        fb[j] = first[:, j * hc:(j + 1) * hc].astype(BF16)
    v2[own, u * TR + slot] = fb[r]
    gz = []
    for j in range(R):
        rr = lax.rem(r + j, R)
        for k in range(B):
            if k or j:
                i = j * B + k - 1
                c = copy(fb.at[rr], v2.at[own, u * TR + slot], g_send.at[i], g_recv.at[i], zpeer(k), t, rr)
                c.start()
                gz.append(c)

    def tile(*values):
        row = lax.broadcasted_iota(jnp.int32, (8, 128), 0)
        x = jnp.zeros((8, 128), F32)
        for i, value in enumerate(values):
            x = jnp.where(row == i, value, x)
        return x

    def spread(buf, index, base, n, to):
        out = []
        for k in range(1, n):
            c = copy(buf.at[index], buf.at[index], sc_send.at[base, k - 1], sc_recv.at[base, k - 1], *to(k))
            c.start()
            out.append(c)
        return out

    def to_slot(k):
        tt, rr = speer(k)
        return b, tt, rr

    def to_blk(k):
        return zpeer(k), t, r

    sc_a[slot] = tile(jnp.sum(start * start), jnp.sum(start * first), jnp.sum(first * first))
    s1 = spread(sc_a, slot, 0, TR, to_slot)

    gx = []
    for k in range(B):
        src = zfrom(k)
        for j in range(R):
            if k or j:
                i = j * B + k - 1
                rr = lax.rem(r - j + R, R)
                there = v2.at[src // 2, (src % 2) * TR + t * R + rr]
                copy(there, there, g_send.at[i], g_recv.at[i], src, t, rr).wait_recv()
        here = piece(v2, src, t * R, R)
        for j in range(1, T):
            c = copy(here, here, gx_send.at[k, j - 1], gx_recv.at[k, j - 1], b, lax.rem(t + j, T), r)
            c.start()
            gx.append(c)
    await_all(s1)
    total = sc_a[0]
    for i in range(1, TR):
        total = total + sc_a[i]
    sc_b[b] = total
    s2 = spread(sc_b, b, 1, B, to_blk)
    for k in range(B):
        src = zfrom(k)
        for j in range(1, T):
            tt = lax.rem(t - j + T, T)
            there = piece(v2, src, tt * R, R)
            copy(there, there, gx_send.at[k, j - 1], gx_recv.at[k, j - 1], b, tt, r).wait_recv()

    halfway(v2)
    p2 = []
    for i in range(2):
        h = u if i == 0 else 1 - u
        x = product(h, 0, 2 * qc)
        for c in range(2):
            part2[2 * h + c] = x[:, c * qc:(c + 1) * qc]
            p2 += scatter(part2, red2, p2_send, p2_recv, 2 * h + c, 2 * i + c)

    await_all(s2)
    total = sc_b[0]
    for i in range(1, B):
        total = total + sc_b[i]

    def row_value(x, i):
        return x[i:i + 1, 0:1]

    self_product, cross, square = row_value(total, 0), row_value(total, 1), row_value(total, 2)
    rayleigh = cross / (self_product + EPSILON)
    residual_square = jnp.maximum(square - 2.0 * rayleigh * cross + rayleigh * rayleigh * self_product, 0.0)
    entries = float(blocks * M * M)
    scale = lax.rsqrt(residual_square / entries + EPSILON)
    first = f_ref[...]
    nb = ((first - rayleigh * start) * scale).astype(BF16)
    nb_out[...] = nb

    await_all(p2)
    second = gathered(part2, red2)
    image = (second - rayleigh * f_ref[...]) * scale
    img_out[...] = image.astype(BF16)
    sc_c[slot] = tile(jnp.sum(nb.astype(F32) * image))
    await_all(spread(sc_c, slot, 2, TR, to_slot))
    total = sc_c[0]
    for i in range(1, TR):
        total = total + sc_c[i]
    sc_d[b] = total
    await_all(spread(sc_d, b, 3, B, to_blk))
    total = sc_d[0]
    for i in range(1, B):
        total = total + sc_d[i]
    lane = lax.broadcasted_iota(jnp.int32, (8, 128), 1)
    proj_out[...] = jnp.where(lane == 0, rayleigh, row_value(total, 0) / entries)
    for c in vz + vx + gz + gx:
        c.wait_send()


def local(wavefunction, left_env, right_env, sources, live_dims):
    B, T, R = lax.axis_size("blk"), lax.axis_size("term"), lax.axis_size("rep")
    TR = T * R
    rows, W, M = left_env.shape
    hc = M // R
    ro = rows // TR
    qc = M // 4
    blocks = live_dims.shape[0]
    vmem = pl.BlockSpec(memory_space=pltpu.VMEM)
    smem = pl.BlockSpec(memory_space=pltpu.SMEM)
    anyw = pl.BlockSpec(memory_space=pl.ANY)
    dma = pltpu.SemaphoreType.DMA
    V = pltpu.VMEM
    nb, img, proj = pl.pallas_call(
        functools.partial(kernel, B, T, R, blocks),
        out_shape=(
            jax.ShapeDtypeStruct((ro, M), BF16),
            jax.ShapeDtypeStruct((ro, M), BF16),
            jax.ShapeDtypeStruct((8, 128), F32),
        ),
        in_specs=[vmem, anyw, anyw, smem, smem],
        out_specs=(vmem, vmem, vmem),
        scratch_shapes=[
            V((rows, W, M), BF16), V((rows, W, M), F32), V((W, rows, M), BF16),
            V((rows, W, hc), BF16), V((rows, W, hc), BF16), V((rows, W, hc), F32),
            V((2, rows, W * hc), BF16),
            V((blocks, 2 * TR, ro, hc), BF16), V((blocks, 2 * TR, ro, hc), BF16), V((blocks, 2 * TR, ro, hc), BF16),
            V((ro, hc), BF16), V((rows, W * hc), BF16),
            V((4, rows, qc), F32), V((4, rows, qc), F32),
            V((4, TR - 1, ro, qc), F32), V((4, TR - 1, ro, qc), F32),
            V((ro, M), F32), V((R, ro, hc), BF16),
            V((TR, 8, 128), F32), V((B, 8, 128), F32), V((TR, 8, 128), F32), V((B, 8, 128), F32),
            dma((2,)), dma((2,)), dma((2,)), dma((B - 1,)), dma((B - 1,)), dma((B - 1, T - 1)), dma((B - 1, T - 1)), dma((2,)),
            dma((4, TR - 1)), dma((4, TR - 1)), dma((4, TR - 1)), dma((4, TR - 1)),
            dma((R * B - 1,)), dma((R * B - 1,)), dma((B, T - 1)), dma((B, T - 1)),
            dma((4, max(TR, B) - 1)), dma((4, max(TR, B) - 1)),
        ],
        compiler_params=pltpu.CompilerParams(collective_id=0, has_side_effects=True, vmem_limit_bytes=50 * 2**20),
    )(wavefunction.reshape(TR, ro, hc), left_env, right_env, sources, live_dims)
    return nb, img, proj[0, :2]


def solution(mesh):
    return jax.shard_map(
        local,
        mesh=mesh,
        in_specs=(
            P(("groups", "blk"), "rep"),
            P(("groups", "blk"), "term", None),
            P(("groups", "blk"), "term", "rep"),
            P("groups", None),
            P("groups", None),
        ),
        out_specs=(
            P(("groups", "blk", "term", "rep"), None),
            P(("groups", "blk", "term", "rep"), None),
            P("groups"),
        ),
        check_vma=False,
    )
```

```python
import functools

import jax
import jax.numpy as jnp
from jax import lax
from jax.experimental import pallas as pl
from jax.experimental.pallas import tpu as pltpu
from jax.sharding import PartitionSpec as P

EPSILON = 1e-06
MESH = pl.DeviceIdType.MESH
F32 = jnp.float32
BF16 = jnp.bfloat16


def kernel(
    B, T, R, blocks,
    wf, left, right, sources, live,
    nb_out, img_out, proj_out,
    left_raw, left_f, left_w, right_raw, right_got, right_f, right_w,
    v1, vm, v2, sbuf, half, part1, part2, red1, red2, f_ref, fb, sc_a, sc_b,
    loc_sem, rsend, rrecv, v_send, v_recv, vx_send, vx_recv, s_sem,
    p1_send, p1_recv, p2_send, p2_recv, g_send, g_recv, gx_send, gx_recv,
    sc_send, sc_recv,
):
    TR = T * R
    b, t, r = lax.axis_index("blk"), lax.axis_index("term"), lax.axis_index("rep")
    slot = t * R + r
    N = B * TR
    me = b * TR + slot
    rows, W, M = left.shape
    ro = rows // TR
    hc = M // R
    qc = M // 4
    own, u = b // 2, b % 2

    def copy(src, dst, ss, rs, bb, tt, rr):
        return pltpu.make_async_remote_copy(
            src_ref=src, dst_ref=dst, send_sem=ss, recv_sem=rs,
            device_id={"blk": bb, "term": tt, "rep": rr}, device_id_type=MESH)

    def zpeer(k):
        p, bit = b, 1
        while bit < B:
            if k & bit:
                p = p + bit - 2 * bit * (b // bit % 2)
            bit *= 2
        return p

    zfrom = zpeer

    def speer(k):
        p = lax.rem(slot + k, TR)
        return p // R, lax.rem(p, R)

    def peer(k):
        p = lax.rem(me + k, N)
        q = lax.rem(p, TR)
        return {"blk": p // TR, "term": q // R, "rep": lax.rem(q, R)}

    barrier = pltpu.get_barrier_semaphore()

    @pl.loop(1, N)
    def _(k):
        pl.semaphore_signal(barrier, inc=1, device_id=peer(k), device_id_type=MESH)

    lcopy = pltpu.make_async_copy(left, left_raw, loc_sem.at[0])
    lcopy.start()
    rcopy = pltpu.make_async_copy(right, right_raw, loc_sem.at[1])
    rcopy.start()
    wcopy = pltpu.make_async_copy(wf, v1.at[own, pl.ds(u * TR, TR)], loc_sem.at[2])
    wcopy.start()
    pl.semaphore_wait(barrier, N - 1)

    def piece(buf, bb, start, n):
        return buf.at[bb // 2, pl.ds((bb % 2) * TR + start, n)]

    vz = []
    for k in range(1, B):
        c = copy(wf.at[pl.ds(t * R, R)], piece(v1, b, t * R, R), v_send.at[k - 1], v_recv.at[k - 1], zpeer(k), t, r)
        c.start()
        vz.append(c)
    mine = [copy(wf.at[t * R + lax.rem(r + 1, R)], sbuf, s_sem.at[0], s_sem.at[1], b, t, lax.rem(r + 1, R))]
    mine[0].start()
    other = b + 1 - 2 * u
    chunk = rows // 4
    rz = []
    for c in range(4):
        d = pl.ds(c * chunk, chunk)
        cp = copy(right.at[d], right_got.at[d], rsend.at[c], rrecv.at[c], other, t, r)
        cp.start()
        rz.append(cp)

    lcopy.wait()
    left_f[...] = left_raw[...].astype(F32)
    for w in range(W):
        left_w[w] = left_f[:, w, :].astype(BF16)
    vx = []
    for k in range(1, B):
        src = zfrom(k)
        here = piece(v1, src, t * R, R)
        copy(here, here, v_send.at[k - 1], v_recv.at[k - 1], src, t, r).wait_recv()
        for j in range(1, T):
            c = copy(here, here, vx_send.at[k - 1, j - 1], vx_recv.at[k - 1, j - 1], b, lax.rem(t + j, T), r)
            c.start()
            vx.append(c)
    rcopy.wait()
    right_f[...] = right_raw[...].astype(F32)
    for w in range(W):
        right_w[u, :, w * hc:(w + 1) * hc] = right_f[:, w, :].astype(BF16)

    for k in range(1, B):
        src = zfrom(k)
        for j in range(1, T):
            tt = lax.rem(t - j + T, T)
            there = piece(v1, src, tt * R, R)
            copy(there, there, vx_send.at[k - 1, j - 1], vx_recv.at[k - 1, j - 1], b, tt, r).wait_recv()
    wcopy.wait()
    row_of = lax.broadcasted_iota(jnp.int32, (2 * TR, ro, hc), 0) * ro + lax.broadcasted_iota(jnp.int32, (2 * TR, ro, hc), 1)
    col_of = lax.broadcasted_iota(jnp.int32, (2 * TR, ro, hc), 2) + r * hc

    @pl.loop(0, blocks)
    def _(k):
        ok = (row_of < live[k, 0]) & (col_of < live[k, 1])
        vm[k] = jnp.where(ok, v1[k].astype(F32), 0.0).astype(BF16)

    def halfway(v):
        for w in range(W):
            src = sources[own, t * W + w]
            x = v[src].reshape(M, hc)
            half[:, w * hc:(w + 1) * hc] = jnp.dot(left_w[w], x, preferred_element_type=F32).astype(BF16)

    def product(h, lo, n):
        return lax.dot_general(half[...], right_w[h, lo:lo + n, :], (((1,), (1,)), ((), ())), preferred_element_type=F32)

    def scatter(part, red, sends, recvs, q, p):
        out = []
        for k in range(1, TR):
            tt, rr = speer(k)
            c = copy(part.at[q, pl.ds(lax.rem(slot + k, TR) * ro, ro)], red.at[q, k - 1],
                     sends.at[p, k - 1], recvs.at[p, k - 1], b, tt, rr)
            c.start()
            out.append(c)
        return out

    out_row = lax.broadcasted_iota(jnp.int32, (ro, M), 0) + u * rows + slot * ro
    out_col = lax.broadcasted_iota(jnp.int32, (ro, M), 1)
    out_live = (out_row < live[own, 0]) & (out_col < live[own, 1])

    def gathered(part, red):
        got = []
        for q in range(4):
            x = part[q, pl.ds(slot * ro, ro), :]
            for k in range(1, TR):
                x = x + red[q, k - 1]
            got.append(x)
        return jnp.where(out_live, jnp.concatenate(got, axis=1), 0.0)

    def await_all(copies):
        for c in copies:
            c.wait()

    halfway(vm)
    x = product(u, 0, 2 * qc)
    part1[2 * u] = x[:, :qc]
    part1[2 * u + 1] = x[:, qc:]
    p1 = scatter(part1, red1, p1_send, p1_recv, 2 * u, 0)
    p1 += scatter(part1, red1, p1_send, p1_recv, 2 * u + 1, 1)
    for c in range(4):
        rz[c].wait()
        lo = c * chunk
        right_f[lo:lo + chunk] = right_got[lo:lo + chunk].astype(F32)
        for w in range(W):
            right_w[1 - u, lo:lo + chunk, w * hc:(w + 1) * hc] = right_f[lo:lo + chunk, w, :].astype(BF16)
        if c % 2:
            q = 2 * (1 - u) + c // 2
            part1[q] = product(1 - u, c // 2 * qc, qc)
            p1 += scatter(part1, red1, p1_send, p1_recv, q, 2 + c // 2)

    mine[0].wait()
    kept = v1[own, u * TR + slot]
    for_r0 = jnp.concatenate([kept, sbuf[...]], axis=1).astype(F32)
    for_r1 = jnp.concatenate([sbuf[...], kept], axis=1).astype(F32)
    start = jnp.where(out_live, jnp.where(r == 0, for_r0, for_r1), 0.0)
    await_all(p1)
    first = gathered(part1, red1)
    f_ref[...] = first

    for j in range(R):
        fb[j] = first[:, j * hc:(j + 1) * hc].astype(BF16)
    v2[own, u * TR + slot] = fb[r]
    gz = []
    for k in range(B):
        for j in range(R):
            rr = lax.rem(r + j, R)
            if k or j:
                i = j * B + k - 1
                c = copy(fb.at[rr], v2.at[own, u * TR + slot], g_send.at[i], g_recv.at[i], zpeer(k), t, rr)
                c.start()
                gz.append(c)

    def lane_sums(x):
        y = jnp.sum(x, axis=0, keepdims=True)
        z = y[:, :128]
        for i in range(1, M // 128):
            z = z + y[:, i * 128:(i + 1) * 128]
        return z

    def shared(buf, base, k):
        return pltpu.make_async_remote_copy(
            src_ref=buf.at[me], dst_ref=buf.at[me], send_sem=sc_send.at[base, k - 1], recv_sem=sc_recv.at[base, k - 1],
            device_id=peer(k), device_id_type=MESH)

    def spread(buf, base):
        @pl.loop(1, N)
        def _(k):
            shared(buf, base, k).start()

    def collect(buf, base):
        @pl.loop(1, N)
        def _(k):
            shared(buf, base, k).wait()

        return jnp.sum(jnp.sum(buf[...], axis=0), axis=1, keepdims=True)

    sc_a[me, 0:1] = lane_sums(start * start)
    sc_a[me, 1:2] = lane_sums(start * first)
    sc_a[me, 2:3] = lane_sums(first * first)
    sc_a[me, 3:4] = jnp.zeros((1, 128), F32)
    spread(sc_a, 0)

    def onward(k, j, to):
        src = zfrom(k)
        rr = lax.rem(r - j + R, R)
        at = lax.rem(t - to + T, T)
        sent = v2.at[src // 2, (src % 2) * TR + t * R + rr]
        got = v2.at[src // 2, (src % 2) * TR + at * R + rr]
        go = copy(sent, sent, gx_send.at[k * R + j, to - 1], gx_recv.at[k * R + j, to - 1], b, lax.rem(t + to, T), r)
        came = copy(got, got, gx_send.at[k * R + j, to - 1], gx_recv.at[k * R + j, to - 1], b, at, r)
        return go, came

    for k in range(B):
        src = zfrom(k)
        for j in range(R):
            if k or j:
                i = j * B + k - 1
                rr = lax.rem(r - j + R, R)
                there = v2.at[src // 2, (src % 2) * TR + t * R + rr]
                copy(there, there, g_send.at[i], g_recv.at[i], src, t, rr).wait_recv()
            for to in range(1, T):
                onward(k, j, to)[0].start()
    for k in range(B):
        for j in range(R):
            for to in range(1, T):
                onward(k, j, to)[1].wait_recv()

    halfway(v2)
    p2 = []
    for i in range(2):
        h = u if i == 0 else 1 - u
        x = product(h, 0, 2 * qc)
        for c in range(2):
            part2[2 * h + c] = x[:, c * qc:(c + 1) * qc]
            p2 += scatter(part2, red2, p2_send, p2_recv, 2 * h + c, 2 * i + c)

    total = collect(sc_a, 0)
    self_product, cross, square = total[0:1], total[1:2], total[2:3]
    rayleigh = cross / (self_product + EPSILON)
    residual_square = jnp.maximum(square - 2.0 * rayleigh * cross + rayleigh * rayleigh * self_product, 0.0)
    entries = float(blocks * M * M)
    scale = lax.rsqrt(residual_square / entries + EPSILON)
    first = f_ref[...]
    nb = ((first - rayleigh * start) * scale).astype(BF16)
    nb_out[...] = nb

    await_all(p2)
    second = gathered(part2, red2)
    image = (second - rayleigh * f_ref[...]) * scale
    img_out[...] = image.astype(BF16)
    sc_b[me] = lane_sums(nb.astype(F32) * image)
    spread(sc_b, 1)
    correlation = collect(sc_b, 1) / entries
    lane = lax.broadcasted_iota(jnp.int32, (8, 128), 1)
    proj_out[...] = jnp.where(lane == 0, rayleigh, correlation)
    for c in vz + vx + gz:
        c.wait_send()
    for k in range(B):
        for j in range(R):
            for to in range(1, T):
                onward(k, j, to)[0].wait_send()


def finish(nb, img, proj, nb_out, img_out, proj_out):
    nb_out[...] = nb[...]
    img_out[...] = img[...]
    lane = lax.broadcasted_iota(jnp.int32, (8, 128), 1)
    row = lax.broadcasted_iota(jnp.int32, (8, 128), 0)
    for i in range(2):
        proj_out[i] = jnp.sum(jnp.where((lane == i) & (row == 0), proj[...], 0.0))


def local(wavefunction, left_env, right_env, sources, live_dims):
    B, T, R = lax.axis_size("blk"), lax.axis_size("term"), lax.axis_size("rep")
    TR = T * R
    rows, W, M = left_env.shape
    hc = M // R
    ro = rows // TR
    qc = M // 4
    blocks = live_dims.shape[0]
    vmem = pl.BlockSpec(memory_space=pltpu.VMEM)
    smem = pl.BlockSpec(memory_space=pltpu.SMEM)
    anyw = pl.BlockSpec(memory_space=pltpu.HBM)
    dma = pltpu.SemaphoreType.DMA
    V = pltpu.VMEM
    nb, img, proj = pl.pallas_call(
        functools.partial(kernel, B, T, R, blocks),
        out_shape=(
            jax.ShapeDtypeStruct((ro, M), BF16),
            jax.ShapeDtypeStruct((ro, M), BF16),
            jax.ShapeDtypeStruct((8, 128), F32),
        ),
        in_specs=[anyw, anyw, anyw, smem, smem],
        out_specs=(vmem, vmem, vmem),
        scratch_shapes=[
            V((rows, W, M), BF16), V((rows, W, M), F32), V((W, rows, M), BF16),
            V((rows, W, hc), BF16), V((rows, W, hc), BF16), V((rows, W, hc), F32),
            V((2, rows, W * hc), BF16),
            V((blocks, 2 * TR, ro, hc), BF16), V((blocks, 2 * TR, ro, hc), BF16), V((blocks, 2 * TR, ro, hc), BF16),
            V((ro, hc), BF16), V((rows, W * hc), BF16),
            V((4, rows, qc), F32), V((4, rows, qc), F32),
            V((4, TR - 1, ro, qc), F32), V((4, TR - 1, ro, qc), F32),
            V((ro, M), F32), V((R, ro, hc), BF16),
            V((B * TR, 4, 128), F32), V((B * TR, 1, 128), F32),
            dma((3,)), dma((4,)), dma((4,)), dma((B - 1,)), dma((B - 1,)), dma((B - 1, T - 1)), dma((B - 1, T - 1)), dma((2,)),
            dma((4, TR - 1)), dma((4, TR - 1)), dma((4, TR - 1)), dma((4, TR - 1)),
            dma((R * B - 1,)), dma((R * B - 1,)), dma((B * R, T - 1)), dma((B * R, T - 1)),
            dma((2, B * TR - 1)), dma((2, B * TR - 1)),
        ],
        compiler_params=pltpu.CompilerParams(collective_id=0, has_side_effects=True, vmem_limit_bytes=62 * 2**20),
    )(wavefunction.reshape(TR, ro, hc), left_env, right_env, sources.T, live_dims)
    return pl.pallas_call(
        finish,
        out_shape=(
            jax.ShapeDtypeStruct((ro, M), BF16),
            jax.ShapeDtypeStruct((ro, M), BF16),
            jax.ShapeDtypeStruct((2,), F32),
        ),
        in_specs=[vmem, vmem, vmem],
        out_specs=(vmem, vmem, smem),
    )(nb, img, proj)


def solution(mesh):
    return jax.shard_map(
        local,
        mesh=mesh,
        in_specs=(
            P(("groups", "blk"), "rep"),
            P(("groups", "blk"), "term", None),
            P(("groups", "blk"), "term", "rep"),
            P("groups", None),
            P("groups", None),
        ),
        out_specs=(
            P(("groups", "blk", "term", "rep"), None),
            P(("groups", "blk", "term", "rep"), None),
            P("groups"),
        ),
        check_vma=False,
    )
```
